512 devices in a mesh: edata: 64 (over z, y), llm: 8 (over x, core).
Axes of the slice: x: 4, y: 4, z: 16, core: 2. Of those that a mesh axis runs over, the one named last changes fastest.
Arguments:
- grad_rows: bfloat16 [32768, 3200], P(('edata', 'llm')), may hold values from -6 to 6
- row_target: int32 [32768, 1], P(('edata', 'llm')), may hold values from 0 to 63; in each aligned block of 64 rows (0 to 63, 64 to 127, ...) at most 2 rows name the same one
- stored_context: bfloat16 [65536, 2048], P('edata', 'llm'), may hold values from -448 to 448
- block_scale: float32 [65536, 16], P('edata', 'llm'), may hold values from 0.002 to 0.008
- w_out: bfloat16 [2048, 3200], P('llm', 'edata'), may hold values from -0.125 to 0.125
- layer_scale: float32 [3200], replicated, may hold values from 0.3 to 3
Outputs:
- grad_context: bfloat16 [65536, 2048], P('edata', 'llm')
- grad_weight: float32 [3200, 2048], P('edata', 'llm')
- grad_scale: float32 [3200], replicated
The draws below stay inside these ranges and needn't reach their ends.
Inputs may be any that keep to these rules, and one draw needn't show every extreme that they name: `row_target`: among the 64 rows of one device, no encoder device is named by more than 2 rows, and some encoder device is named by exactly 2 rows.
All inputs are finite; a program needn't handle non-finite values.
Results may differ from the reference program's by a relative error of at most 0.0049.
Values may be sent and summed in bfloat16 or wider, within the bound.
No kernel may reach another device: no remote copies, remote signals or barrier semaphores. Data moves between devices by JAX's collectives and lax.ppermute only.
A program may use at most 128 MiB of HBM per device.

```python
import math
import jax
import jax.numpy as jnp
import numpy as np
from jax import lax

WIDTH = 3200
BLOCK = 128
SRC_DEV = 64
CTX = 2048
CAP = 2
SLOTS = 1024
ROWS = 32768
N_EDATA = 64
N_LLM = 8


def steps_of(own_key, extent, pieces, smallest, top_value):
    gain, own = 1.0, jax.random.fold_in(own_key, 6)
    for position, blocks in pieces:
        heights = jnp.exp(jax.random.uniform(jax.random.fold_in(own, position), (blocks,), jnp.float32, smallest / len(pieces), top_value / len(pieces)))
        gain = gain * jnp.repeat(heights, extent[position] // blocks).reshape([-1 if axis == position else 1 for axis in range(len(extent))])
    return gain


def shared_out(key, own, number, rows, number_of, top, reach, slope):
    ranking = jax.random.permutation(key, number_of)
    heavy_load, usual = portions_of(number_of, rows * top, reach, slope, True), portions_of(number_of, rows * top, reach, slope, False)
    places = jnp.arange(number_of)

    def named(sizes, offset_by):
        used = int((sizes > 0).sum())
        fixed = max(1, used // 4)
        passed = fixed + (places - fixed + offset_by * (used - fixed)) % max(1, number_of - fixed)
        return jnp.zeros((number_of,), jnp.int32).at[ranking[jnp.where(places < fixed, places, passed)]].set(jnp.asarray(sizes, jnp.int32))

    sizes = jnp.where(number % 4 == 0, named(heavy_load, number // 4), named(usual, number - number // 4 - 1))
    mixed = jax.random.permutation(jax.random.fold_in(own, 3), number_of)
    source_of, receiver = mixed[0:number_of // 2 * 2:2], mixed[1:number_of // 2 * 2:2]
    slack = jnp.minimum(sizes[source_of] - 1, reach - sizes[receiver]) // 2
    slack = jnp.where((source_of == ranking[0]) | (receiver == ranking[0]) | (sizes[receiver] == 0), 0, jnp.maximum(slack, 0))
    passed = jax.random.randint(jax.random.fold_in(own, 4), (number_of // 2,), 0, 1 << 20) % (slack + 1)
    sizes = sizes.at[source_of].add(-passed).at[receiver].add(passed)
    labels = jnp.searchsorted(jnp.cumsum(sizes), jnp.arange(rows * top), side="right").astype(jnp.int32)
    grid = labels.reshape(top, rows).T
    grid = grid[jax.random.permutation(jax.random.fold_in(own, 1), rows)]
    offset_by = jax.random.randint(jax.random.fold_in(own, 2), (rows, 1), 0, top)
    return jnp.take_along_axis(grid, (jnp.arange(top)[None, :] + offset_by) % top, axis=1)


def portions_of(number_of, total, reach, lean, full):
    portions = [(1 << 20) // math.isqrt(rank ** lean) + 1 for rank in range(1, number_of + 1)]
    largest = reach if full else min(reach, max(-(-total // number_of), total * portions[0] // sum(portions)))
    least = 1 if total - largest >= number_of - 1 else 0
    given, surplus = [largest] + [least] * (number_of - 1), total - largest - least * (number_of - 1)
    while surplus > 0:
        candidates = [i for i in range(1, number_of) if given[i] < largest] or [i for i in range(1, number_of) if given[i] < reach]
        mass, budget = sum([portions[i] for i in candidates]), surplus
        for i in candidates:
            addition = min(reach - given[i], max(1, budget * portions[i] // mass), surplus)
            given[i] = given[i] + addition
            surplus = surplus - addition
    return np.array(given)


def noise(stream_key, dims, deviation, reach, shards=(), kind=jnp.bfloat16):
    loudness = steps_of(stream_key, dims, shards, -0.22, 0.18) if shards else 1.0
    array = jax.random.normal(stream_key, dims, jnp.float32) * deviation * loudness
    return jnp.minimum(jnp.maximum(array, -reach), reach).astype(kind)


def setup_inputs(seed: int = 0) -> dict:
    streams_of = jax.random.split(jax.random.key(seed), 7)
    grad_rows = noise(streams_of[0], (ROWS, WIDTH), 1.0, 6.0, ((0, 512),))
    row_target_keys = jax.random.split(jax.random.fold_in(streams_of[1], 1), ROWS // SRC_DEV)
    row_target_turns = jax.random.permutation(jax.random.fold_in(streams_of[1], 3), ROWS // SRC_DEV)
    row_target = jax.vmap(lambda own, number: shared_out(jax.random.fold_in(streams_of[1], 2), own, number, SRC_DEV, N_EDATA, 1, CAP, 2))(row_target_keys, row_target_turns).reshape((ROWS, 1))
    stored_context = jnp.clip(jax.random.uniform(streams_of[2], (N_EDATA * SLOTS, CTX), jnp.float32, -448.0, 448.0) * steps_of(streams_of[2], (N_EDATA * SLOTS, CTX), ((0, 64), (1, 8)), -0.4, 0.0), -448.0, 448.0).astype(jnp.bfloat16)
    block_scale = jnp.clip(jnp.exp(math.log(0.008) - 1.3862944 * jax.random.uniform(streams_of[3], (N_EDATA * SLOTS, CTX // BLOCK), jnp.float32) ** steps_of(streams_of[3], (N_EDATA * SLOTS, CTX // BLOCK), ((0, 64), (1, 8)), -0.2, 0.2)), 0.002, 0.008)
    w_out = noise(streams_of[4], (CTX, WIDTH), CTX ** -0.5, 0.125, ((0, 8), (1, 64)))
    layer_scale = jnp.clip(jnp.exp(jax.random.uniform(streams_of[5], (WIDTH,), jnp.float32, math.log(0.3), math.log(3.0))), 0.3, 3.0)
    return {"grad_rows": grad_rows, "row_target": row_target, "stored_context": stored_context, "block_scale": block_scale, "w_out": w_out, "layer_scale": layer_scale}


def reference(grad_rows, row_target, stored_context, block_scale, w_out, layer_scale):
    targets = row_target[:, 0].reshape(N_EDATA, N_LLM, SRC_DEV)
    chosen = (targets[..., None] == jnp.arange(N_EDATA, dtype=jnp.int32)).astype(jnp.int32)
    arrival = lax.optimization_barrier(jnp.sum(chosen * (jnp.cumsum(chosen, axis=2) - 1), axis=3)).astype(jnp.int32)
    source_enc = jnp.arange(N_EDATA, dtype=jnp.int32)[:, None, None]
    source_own = jnp.arange(N_LLM, dtype=jnp.int32)[None, :, None]
    slot_index = (source_own * N_EDATA + source_enc) * CAP + arrival
    placed = (targets * SLOTS + slot_index).reshape(ROWS).astype(jnp.int32)
    stored = stored_context[placed].astype(jnp.float32).reshape(ROWS, CTX // BLOCK, BLOCK)
    context = (stored * block_scale[placed][:, :, None]).reshape(ROWS, CTX).astype(jnp.bfloat16)
    scaled = (grad_rows.astype(jnp.float32) * layer_scale[None, :]).astype(jnp.bfloat16)
    recomputed = jnp.dot(context, w_out, preferred_element_type=jnp.float32)
    live_grad = jnp.dot(scaled, w_out.T, preferred_element_type=jnp.float32).astype(jnp.bfloat16)
    grad_context = jnp.zeros((N_EDATA * SLOTS, CTX), jnp.bfloat16).at[placed].set(live_grad)
    rescale = 1.0 / math.sqrt(ROWS)
    grad_weight = jnp.dot(scaled.T, context, preferred_element_type=jnp.float32) * rescale
    grad_scale = lax.optimization_barrier(jnp.sum(grad_rows.astype(jnp.float32) * recomputed, axis=0)) * rescale
    return (grad_context, grad_weight, grad_scale)
```

```python
import math

import jax
import jax.numpy as jnp
from jax import lax
from jax.sharding import Mesh
from jax.sharding import PartitionSpec as P

BLOCK = 128
F32 = jnp.float32
BF16 = jnp.bfloat16


def group_pairs(size, group, stride, shift):
    pairs = []
    for i in range(size):
        digit = (i // stride) % group
        pairs.append((i, i + ((digit + shift) % group - digit) * stride))
    return pairs


def exchange(blocks, axis, size, group, stride):
    digit = (lax.axis_index(axis) // stride) % group
    got = [lax.dynamic_index_in_dim(blocks, digit, 0, keepdims=False)]
    for shift in range(1, group):
        block = lax.dynamic_index_in_dim(blocks, (digit + shift) % group, 0, keepdims=False)
        got.append(lax.ppermute(block, axis, group_pairs(size, group, stride, shift)))
    return got


def sum_all(value, axis, size, group, stride):
    total = value
    for shift in range(1, group):
        total = total + lax.ppermute(value, axis, group_pairs(size, group, stride, shift))
    return total


def on_device(grad_rows, row_target, stored_context, block_scale, w_out, layer_scale):
    nz, ny, nx, nc = (lax.axis_size(a) for a in ("z", "y", "x", "c"))
    encoders, owners = nz * ny, nx * nc
    source_rows, features = grad_rows.shape
    slot_count, width = stored_context.shape
    capacity = slot_count // (encoders * owners)
    own = features // encoders

    stored = stored_context.astype(F32).reshape(slot_count, -1, BLOCK)
    context = (stored * block_scale[:, :, None]).reshape(slot_count, width).astype(BF16)
    send = context.reshape(owners, encoders, capacity, width).transpose(1, 0, 2, 3)
    send = send.reshape(encoders, owners * capacity, width)
    slots = lax.all_to_all(send, ("z", "y"), split_axis=0, concat_axis=0, tiled=True)
    slots = slots.reshape(slot_count, width)

    pad = 16
    extra = jnp.zeros((pad, features), BF16).at[0, :source_rows].set(row_target[:, 0].astype(BF16))
    rows = lax.all_gather(jnp.concatenate([grad_rows, extra], axis=0), ("x", "c"), axis=0, tiled=True)
    weights = lax.all_gather(w_out.T, "z", axis=0, tiled=False)
    weights = lax.all_gather(weights, "y", axis=1, tiled=False).reshape(features, width)

    targets = rows.reshape(owners, source_rows + pad, features)[:, source_rows, :source_rows].astype(jnp.int32)
    place = jnp.arange(source_rows, dtype=jnp.int32)
    same = (targets[:, :, None] == targets[:, None, :]) & (place[None, None, :] < place[None, :, None])
    arrival = jnp.sum(same.astype(jnp.int32), axis=2)
    owner = jnp.arange(owners, dtype=jnp.int32)[:, None]
    slot = targets * (owners * capacity) + owner * capacity + arrival
    slot = jnp.pad(slot, ((0, 0), (0, pad)), constant_values=-1).reshape(-1)
    select = (slot[:, None] == jnp.arange(slot_count, dtype=jnp.int32)[None, :]).astype(BF16)

    row_context = jnp.dot(select, slots, preferred_element_type=F32).astype(BF16)
    partial = lax.dot_general(rows, row_context, (((0,), (0,)), ((), ())), preferred_element_type=F32)

    scaled = (rows.astype(F32) * layer_scale[None, :]).astype(BF16)
    live = jnp.dot(scaled, weights, preferred_element_type=F32).astype(BF16)
    back = lax.dot_general(select, live, (((0,), (0,)), ((), ())), preferred_element_type=F32).astype(BF16)
    back = back.reshape(encoders, owners * capacity, width)
    back = lax.all_to_all(back, ("z", "y"), split_axis=0, concat_axis=0, tiled=True)
    back = back.reshape(encoders, owners, capacity, width).transpose(1, 0, 2, 3)
    grad_context = back.reshape(slot_count, width)

    rescale = 1.0 / math.sqrt(source_rows * encoders * owners)
    scale_part = jnp.sum(weights.astype(F32) * partial, axis=1).reshape(features // BLOCK, BLOCK)
    scale_part = sum_all(scale_part, "c", nc, nc, 1)
    scale_part = sum_all(scale_part, "x", nx, nx, 1)
    scale_part = sum_all(scale_part, "y", ny, ny, 1)
    scale_part = sum_all(scale_part, "z", nz, 4, 1)
    scale_part = sum_all(scale_part, "z", nz, nz // 4, 4)
    grad_scale = scale_part.reshape(features) * rescale

    blocks = partial.astype(BF16).reshape(nz, ny, own, width).transpose(1, 0, 2, 3)
    total = sum(b.astype(F32) for b in exchange(blocks, "y", ny, ny, 1))
    blocks = total.astype(BF16).reshape(nz // 4, 4, own, width).transpose(1, 0, 2, 3)
    total = sum(b.astype(F32) for b in exchange(blocks, "z", nz, 4, 1))
    total = sum(exchange(total, "z", nz, nz // 4, 4))
    place = lax.axis_index(("z", "y")) * own
    own_scale = lax.dynamic_slice(layer_scale, (place,), (own,))
    grad_weight = total * (own_scale * rescale)[:, None]
    return (grad_context, grad_weight, grad_scale)


def solution(mesh):
    finer = Mesh(mesh.devices.reshape(16, 4, 4, 2), ("z", "y", "x", "c"))
    edata, llm = ("z", "y"), ("x", "c")
    in_specs = (
        P(edata + llm, None),
        P(edata + llm, None),
        P(edata, llm),
        P(edata, llm),
        P(llm, edata),
        P(),
    )
    out_specs = (P(edata, llm), P(edata, llm), P())
    return jax.shard_map(
        on_device, mesh=finer, in_specs=in_specs, out_specs=out_specs, check_vma=False
    )
```

```python
import math

import jax
import jax.numpy as jnp
from jax import lax
from jax.experimental import pallas as pl
from jax.experimental.pallas import tpu as pltpu
from jax.sharding import Mesh
from jax.sharding import PartitionSpec as P

BLOCK = 128
F32 = jnp.float32
BF16 = jnp.bfloat16
I32 = jnp.int32
Z = ("h", "l")
ROWS_FIRST = (((0,), (0,)), ((), ()))
LANES_LAST = (((1,), (1,)), ((), ()))


def call(kernel, out_shape, args, flops, scalars=0, scratch=(), after=()):
    whole = pl.BlockSpec(memory_space=pltpu.VMEM)
    count, more = len(args), len(after)

    def body(*refs):
        kernel(*refs[:count], *refs[count + more :])

    specs = [pl.BlockSpec(memory_space=pltpu.SMEM)] * scalars + [whole] * (count - scalars)
    return pl.pallas_call(
        body,
        out_shape=out_shape,
        in_specs=specs + [pl.BlockSpec(memory_space=pl.ANY)] * more,
        out_specs=jax.tree.map(lambda _: whole, out_shape),
        scratch_shapes=list(scratch),
        compiler_params=pltpu.CompilerParams(vmem_limit_bytes=48 * 2**20),
        cost_estimate=pl.CostEstimate(flops=flops, bytes_accessed=4 * 2**20, transcendentals=0),
    )(*args, *after)


def swap_matrix(inner, outer, capacity, dtype):
    size = inner * outer * capacity
    row = lax.broadcasted_iota(I32, (size, size), 0)
    col = lax.broadcasted_iota(I32, (size, size), 1)
    o, i, a = row // (inner * capacity), (row // capacity) % inner, row % capacity
    return (col == (i * outer + o) * capacity + a).astype(dtype)


def context_kernel(owners, encoders, capacity, place, stored, scale, *refs):
    sends, send = refs[:-1], refs[-1]
    group = 8
    slab = group * capacity
    matrix = swap_matrix(owners, group, capacity, BF16)
    parts = []
    for b in range(scale.shape[1]):
        part = stored[:, b * BLOCK : (b + 1) * BLOCK].astype(F32) * scale[:, b : b + 1]
        parts.append(part.astype(BF16))
    context = jnp.concatenate(parts, axis=1)
    block = owners * capacity
    for g in range(encoders // group):
        picked = [context[(l * encoders + g * group) * capacity :][:slab] for l in range(owners)]
        moved = jnp.dot(matrix, jnp.concatenate(picked, axis=0), preferred_element_type=F32).astype(BF16)
        for e in range(group):
            z, y = divmod(g * group + e, send.shape[0])
            send[y, z] = moved[e * block : (e + 1) * block, :]
    for k, out in enumerate(sends):
        out[...] = send[lax.rem(place[1] + k, len(sends))]


def rows_kernel(capacity, own_owner, rows, target_col, target_row, mine):
    count, features = rows.shape
    earlier = lax.broadcasted_iota(I32, (count, count), 1) < lax.broadcasted_iota(I32, (count, count), 0)
    same = jnp.where((target_col[...] == target_row[...]) & earlier, 1.0, 0.0)
    arrival = jnp.sum(same, axis=1, keepdims=True)
    low = arrival + (own_owner[0] * capacity).astype(F32)
    lane = lax.broadcasted_iota(I32, (count, BLOCK), 1)
    tail = jnp.where(lane == 0, target_col[...].astype(F32), jnp.where(lane == 1, low, 0.0))
    mine[:, :features] = rows[...]
    mine[:, features:] = tail.astype(BF16)


def stack_kernel(*refs):
    out, count = refs[-1], refs[0].shape[0]
    for k, ref in enumerate(refs[:-1]):
        out[k * count : (k + 1) * count, :] = ref[...]


def selection(tail, per_target, slot_count):
    tail = tail.astype(F32)
    slot = (tail[:, 0:1] * per_target + tail[:, 1:2]).astype(I32)
    lanes = lax.broadcasted_iota(I32, (tail.shape[0], slot_count), 1)
    return (lanes == slot).astype(BF16)


def outer_kernel(nz, ny, per_target, place, slots, *refs):
    gathered, (kept, *sends), (total, ordered) = refs[: -ny - 2], refs[-ny - 2 : -2], refs[-2:]
    features, width = total.shape
    own = features // (nz * ny)
    slot_count = slots.shape[0]
    contexts = []
    for rows in gathered:
        select = selection(rows[:, features:], per_target, slot_count)
        contexts.append(jnp.dot(select, slots[...], preferred_element_type=F32).astype(BF16))
    step = 5 * BLOCK
    for i in range(features // step):
        part = 0.0
        for rows, context in zip(gathered, contexts):
            part += lax.dot_general(rows[:, i * step : (i + 1) * step], context, ROWS_FIRST, preferred_element_type=F32)
        total[i * step : (i + 1) * step, :] = part
    for z in range(nz):
        for y in range(ny):
            ordered[y, z * own : (z + 1) * own, :] = total[(z * ny + y) * own : (z * ny + y + 1) * own, :]
    kept[...] = ordered[place[1]]
    for k, send in enumerate(sends, 1):
        send[...] = ordered[lax.rem(place[1] + k, ny)].astype(BF16)


def back_kernel(nz, ny, per_target, place, scale, w0, w1, w2, w3, *refs):
    gathered, (out, wide, weights) = refs[:-3], refs[-3:]
    features, width = weights.shape
    own = features // (nz * ny)
    here_y = place[1]
    for k, piece in enumerate((w0, w1, w2, w3)):
        y = lax.rem(here_y + ny - k, ny)
        wide[pl.ds(y, 1)] = piece[...].astype(F32)[None]
    for z in range(nz):
        for y in range(ny):
            at = (z * ny + y) * own
            weights[at : at + own, :] = wide[y, z]
    slot_count = out.shape[0]
    step = 5 * BLOCK
    total = jnp.zeros((slot_count, width), F32)
    for rows in gathered:
        live = jnp.zeros((rows.shape[0], width), F32)
        for i in range(features // step):
            cut = slice(i * step, (i + 1) * step)
            scaled = (rows[:, cut].astype(F32) * scale[:, cut]).astype(BF16)
            live += jnp.dot(scaled, weights[cut, :].astype(BF16), preferred_element_type=F32)
        select = selection(rows[:, features:], per_target, slot_count)
        total += lax.dot_general(select, live.astype(BF16), ROWS_FIRST, preferred_element_type=F32)
    out[...] = total.astype(BF16)


def both_terms(value):
    high = value.astype(BF16).astype(F32)
    return jnp.concatenate([high, value - high], axis=0).astype(BF16)


def fold_y_kernel(nz, own, groups, place, kept, r1, r2, r3, by_z, near_kept, scale_kept, *rest):
    sends, (blocks, product) = rest[:-2], rest[-2:]
    padded = product.shape[0] // nz
    width = product.shape[1]
    members = nz // groups
    total = kept[...]
    for part in (r1, r2, r3):
        total += part[...].astype(F32)
    product[...] = jnp.zeros_like(product)
    for z in range(nz):
        block = total[z * own : (z + 1) * own, :]
        blocks[z] = block
        weight = by_z[z].astype(F32)
        product[z * padded : z * padded + own, :] = block * weight
    rest = product[...]
    ones = jnp.ones((8, width), BF16)
    sums = jnp.zeros((8, nz * padded), F32)
    for _ in range(3):
        piece = rest.astype(BF16)
        rest = rest - piece.astype(F32)
        sums += lax.dot_general(ones, piece, LANES_LAST, preferred_element_type=F32)
    scale_kept[...] = jnp.zeros_like(scale_kept)
    for j in range(-(-nz * padded // width)):
        row = sums[0:1, j * width : (j + 1) * width]
        scale_kept[j : j + 1, : row.shape[1]] = row
    both = both_terms(scale_kept[...])
    low = lax.rem(place[0], members)
    for h in range(groups):
        near_kept[h] = blocks[h * members + low]
    for k, send in enumerate(sends, 1):
        there = lax.rem(low + k, members)
        for h in range(groups):
            send[h] = blocks[h * members + there].astype(BF16)
        send[groups] = jnp.zeros_like(send[groups])
        send[groups, : both.shape[0], :] = both


def fold_low_kernel(near_kept, scale_kept, r1, r2, r3, out):
    groups, own, width = near_kept.shape
    lines = scale_kept.shape[0]
    scale = scale_kept[...]
    for part in (r1, r2, r3):
        both = part[groups, : 2 * lines, :].astype(F32)
        scale = scale + (both[:lines] + both[lines:])
    for h in range(groups):
        total = near_kept[h]
        for part in (r1, r2, r3):
            total += part[h].astype(F32)
        out[h, :own, :] = total
        out[h, own : out.shape[1] - lines, :] = jnp.zeros((out.shape[1] - lines - own, width), F32)
        out[h, out.shape[1] - lines :, :] = scale


def fold_high_kernel(factor, parts, gain, out, scale_out):
    total = parts[0]
    for h in range(1, parts.shape[0]):
        total += parts[h]
    own, lines = out.shape[0], scale_out.shape[1]
    out[...] = total[:own] * (gain[...] * factor)
    for k in range(scale_out.shape[0]):
        scale_out[k] = total[total.shape[0] - lines :]


def spread_kernel(source, out):
    for k in range(out.shape[0]):
        out[k] = source[...]


def collect_kernel(place, *refs):
    parts, out = refs[:-1], refs[-1]
    for k, part in enumerate(parts):
        y = lax.rem(place[1] + len(parts) - k, len(parts))
        for z in range(out.shape[0]):
            out[z, y] = part[z]


def share_kernel(place, source, kept, *sends):
    count = source.shape[1]
    for k, out in enumerate((kept,) + sends):
        there = lax.rem(place[1] + k, count)
        for z in range(source.shape[0]):
            out[z] = source[z, there]


def unswap_kernel(owners, capacity, place, *refs):
    parts, (out, ordered) = refs[:-2], refs[-2:]
    ny, nz, width = len(parts), ordered.shape[0], ordered.shape[3]
    encoders = nz * ny
    for k, part in enumerate(parts):
        y = lax.rem(place[1] + ny - k, ny)
        for z in range(nz):
            ordered[z, y] = part[z]
    group = 8
    slab = group * capacity
    matrix = swap_matrix(group, owners, capacity, BF16)
    for g in range(encoders // group):
        picked = [ordered[(g * group + e) // ny, (g * group + e) % ny] for e in range(group)]
        moved = jnp.dot(matrix, jnp.concatenate(picked, axis=0), preferred_element_type=F32).astype(BF16)
        for l in range(owners):
            at = (l * encoders + g * group) * capacity
            out[at : at + slab, :] = moved[l * slab : (l + 1) * slab, :]


def shifted(value, axis, size, shift):
    return lax.ppermute(value, axis, [(i, (i + shift) % size) for i in range(size)])


def all_to_all(value, axes):
    return lax.all_to_all(value, axes, split_axis=0, concat_axis=0, tiled=True)


def on_device(grad_rows, row_target, stored_context, block_scale, w_out, layer_scale):
    nz, ny, nx, nc = (lax.axis_size(a) for a in (Z, "y", "x", "c"))
    encoders, owners = nz * ny, nx * nc
    source_rows, features = grad_rows.shape
    slot_count, width = stored_context.shape
    capacity = slot_count // (encoders * owners)
    own = features // encoders
    per_target = owners * capacity
    shape = jax.ShapeDtypeStruct
    owner = lax.axis_index(("x", "c")).reshape(1)
    place = jnp.stack([lax.axis_index(Z), lax.axis_index("y")])

    send = call(
        lambda *args: context_kernel(owners, encoders, capacity, *args),
        [shape((nz, per_target, width), BF16)] * ny, (place, stored_context, block_scale), flops=10**8, scalars=1,
        scratch=[pltpu.VMEM((ny, nz, per_target, width), BF16)],
    )
    weights = all_to_all(
        call(spread_kernel, shape((nz, own, width), BF16), (w_out.T,), flops=10**6, after=(send[0],)), Z,
    )
    sent = [send[0]] + [shifted(part, "y", ny, k) for k, part in enumerate(send[1:], 1)]
    received = sent[1:]
    sent = call(
        collect_kernel, shape((nz, ny, per_target, width), BF16), (place, *sent), flops=10**8, scalars=1, after=(weights,),
    )
    slots = all_to_all(sent, Z).reshape(slot_count, width)

    wide = features + BLOCK
    mine = call(
        lambda *args: rows_kernel(capacity, *args),
        shape((source_rows, wide), BF16), (owner, grad_rows, row_target, row_target.reshape(1, source_rows)),
        flops=10**8, scalars=1, after=received,
    )
    near = call(
        stack_kernel, shape((nx * source_rows, wide), BF16), [mine] + [shifted(mine, "x", nx, k) for k in range(1, nx)],
        flops=10**8, after=(weights,),
    )
    rows = [near, shifted(near, "c", nc, 1)]
    pieces = [weights] + [shifted(weights, "y", ny, k) for k in range(1, ny)]

    share = nz * own
    kept, *sends = call(
        lambda *args: outer_kernel(nz, ny, per_target, *args),
        [shape((share, width), F32)] + [shape((share, width), BF16)] * (ny - 1),
        (place, slots, *rows), flops=10**9, scalars=1,
        scratch=[pltpu.VMEM((features, width), F32), pltpu.VMEM((ny, share, width), F32)],
    )
    parts = [shifted(send, "y", ny, k) for k, send in enumerate(sends, 1)]

    back = call(
        lambda *args: back_kernel(nz, ny, per_target, *args),
        shape((slot_count, width), BF16),
        (place, layer_scale.reshape(1, features), *pieces, *rows), flops=2 * 10**9, scalars=1, after=(kept,),
        scratch=[pltpu.VMEM((ny, nz, own, width), F32), pltpu.VMEM((features, width), F32)],
    )
    returned = all_to_all(back.reshape(nz, ny, per_target, width), Z)
    sends = call(
        share_kernel, [shape((nz, per_target, width), BF16)] * ny, (place, returned), flops=10**8, scalars=1,
    )
    sends = [sends[0]] + [shifted(send, "y", ny, k) for k, send in enumerate(sends[1:], 1)]
    grad_context = call(
        lambda *args: unswap_kernel(owners, capacity, *args),
        shape((slot_count, width), BF16), (place, *sends), flops=10**8, scalars=1,
        scratch=[pltpu.VMEM((nz, ny, per_target, width), BF16)],
    )

    groups = lax.axis_size("h")
    members = nz // groups
    padded = -(-own // 8) * 8
    lines = -(-nz * padded // width)
    low, low_scale, *sends = call(
        lambda *args: fold_y_kernel(nz, own, groups, *args),
        [shape((groups, own, width), F32), shape((lines, width), F32)]
        + [shape((groups + 1, own, width), BF16)] * (members - 1),
        (place, kept, *parts, weights), flops=2 * 10**11, scalars=1,
        scratch=[pltpu.VMEM((nz, own, width), F32), pltpu.VMEM((nz * padded, width), F32)],
    )
    parts = [shifted(send, "l", members, k) for k, send in enumerate(sends, 1)]
    rows_sent = -(-(own + lines) // 8) * 8
    total = call(
        fold_low_kernel, shape((groups, rows_sent, width), F32), (low, low_scale, *parts), flops=10**11, after=(returned,),
    )
    rescale = 1.0 / math.sqrt(source_rows * encoders * owners)
    at = lax.axis_index(Z + ("y",)) * own
    own_scale = lax.dynamic_slice(layer_scale, (at,), (own,))
    grad_weight, scale_part = call(
        lambda *args: fold_high_kernel(rescale, *args),
        [shape((own, width), F32), shape((ny * owners, lines, width), F32)],
        (all_to_all(total, "h"), own_scale.reshape(own, 1)), flops=10**8,
    )
    scale_part = all_to_all(scale_part, ("y", "x", "c")).reshape(ny, owners, lines * width)[:, :, : nz * padded]
    scale_part = jnp.sum(scale_part, axis=1).reshape(ny, nz, padded)[:, :, :own]
    grad_scale = scale_part.transpose(1, 0, 2).reshape(features) * rescale
    return (grad_context, grad_weight, grad_scale)


def solution(mesh):
    finer = Mesh(mesh.devices.reshape(4, 4, 4, 4, 2), Z + ("y", "x", "c"))
    edata, llm = Z + ("y",), ("x", "c")
    in_specs = (
        P(edata + llm, None),
        P(edata + llm, None),
        P(edata, llm),
        P(edata, llm),
        P(llm, edata),
        P(),
    )
    out_specs = (P(edata, llm), P(edata, llm), P())
    return jax.shard_map(
        on_device, mesh=finer, in_specs=in_specs, out_specs=out_specs, check_vma=False
    )
```

```python
import math

import jax
import jax.numpy as jnp
from jax import lax
from jax.experimental import pallas as pl
from jax.experimental.pallas import tpu as pltpu
from jax.sharding import Mesh
from jax.sharding import PartitionSpec as P

BLOCK = 128
F32 = jnp.float32
BF16 = jnp.bfloat16
I32 = jnp.int32
Z = ("h", "l")
ROWS_FIRST = (((0,), (0,)), ((), ()))
LANES_LAST = (((1,), (1,)), ((), ()))


def call(kernel, out_shape, args, flops, scalars=0, scratch=(), after=()):
    whole = pl.BlockSpec(memory_space=pltpu.VMEM)
    count, more = len(args), len(after)

    def body(*refs):
        kernel(*refs[:count], *refs[count + more :])

    specs = [pl.BlockSpec(memory_space=pltpu.SMEM)] * scalars + [whole] * (count - scalars)
    return pl.pallas_call(
        body,
        out_shape=out_shape,
        in_specs=specs + [pl.BlockSpec(memory_space=pl.ANY)] * more,
        out_specs=jax.tree.map(lambda _: whole, out_shape),
        scratch_shapes=list(scratch),
        compiler_params=pltpu.CompilerParams(vmem_limit_bytes=20 * 2**20),
        cost_estimate=pl.CostEstimate(flops=flops, bytes_accessed=4 * 2**20, transcendentals=0),
    )(*args, *after)


def for_each(index, count, body):
    for value in range(count):

        @pl.when(index == value)
        def _(value=value):
            body(value)


def swap_matrix(inner, outer, capacity, dtype):
    size = inner * outer * capacity
    row = lax.broadcasted_iota(I32, (size, size), 0)
    col = lax.broadcasted_iota(I32, (size, size), 1)
    o, i, a = row // (inner * capacity), (row // capacity) % inner, row % capacity
    return (col == (i * outer + o) * capacity + a).astype(dtype)


def context_kernel(owners, encoders, capacity, place, stored, scale, *refs):
    sends, send = refs[:-1], refs[-1]
    group = 8
    slab = group * capacity
    matrix = swap_matrix(owners, group, capacity, BF16)
    parts = []
    for b in range(scale.shape[1]):
        part = stored[:, b * BLOCK : (b + 1) * BLOCK].astype(F32) * scale[:, b : b + 1]
        parts.append(part.astype(BF16))
    context = jnp.concatenate(parts, axis=1)
    block = owners * capacity
    for g in range(encoders // group):
        picked = [context[(l * encoders + g * group) * capacity :][:slab] for l in range(owners)]
        moved = jnp.dot(matrix, jnp.concatenate(picked, axis=0), preferred_element_type=F32).astype(BF16)
        for e in range(group):
            z, y = divmod(g * group + e, send.shape[0])
            send[y, z] = moved[e * block : (e + 1) * block, :]
    for k, out in enumerate(sends):
        out[...] = send[lax.rem(place[1] + k, len(sends))]


def rows_kernel(capacity, own_owner, rows, target_col, target_row, mine):
    count, features = rows.shape
    earlier = lax.broadcasted_iota(I32, (count, count), 1) < lax.broadcasted_iota(I32, (count, count), 0)
    same = jnp.where((target_col[...] == target_row[...]) & earlier, 1.0, 0.0)
    arrival = jnp.sum(same, axis=1, keepdims=True)
    low = arrival + (own_owner[0] * capacity).astype(F32)
    lane = lax.broadcasted_iota(I32, (count, BLOCK), 1)
    tail = jnp.where(lane == 0, target_col[...].astype(F32), jnp.where(lane == 1, low, 0.0))
    mine[:, :features] = rows[...]
    mine[:, features:] = tail.astype(BF16)


def stack_kernel(*refs):
    out, count = refs[-1], refs[0].shape[0]
    for k, ref in enumerate(refs[:-1]):
        out[k * count : (k + 1) * count, :] = ref[...]


def selection(tail, per_target, slot_count):
    tail = tail.astype(F32)
    slot = (tail[:, 0:1] * per_target + tail[:, 1:2]).astype(I32)
    lanes = lax.broadcasted_iota(I32, (tail.shape[0], slot_count), 1)
    return (lanes == slot).astype(BF16)


def outer_kernel(nz, ny, per_target, place, slots, *refs):
    gathered, (kept, *sends), ordered = refs[: -ny - 1], refs[-ny - 1 : -1], refs[-1]
    share, width = kept.shape
    features, own = share * ny, share // nz
    selects = [selection(rows[:, features:], per_target, slots.shape[0]) for rows in gathered]
    contexts = [jnp.dot(select, slots[...], preferred_element_type=F32).astype(BF16) for select in selects]
    step = 5 * BLOCK
    for at in range(0, features, step):
        part = 0.0
        for rows, context in zip(gathered, contexts):
            part += lax.dot_general(rows[:, at : at + step], context, ROWS_FIRST, preferred_element_type=F32)
        first = at
        while first < at + step:
            block, row = divmod(first, own)
            count = min(own - row, at + step - first)
            z, y = divmod(block, ny)
            ordered[y, z * own + row : z * own + row + count, :] = part[first - at : first - at + count, :]
            first += count

    def hand_out(y):
        kept[...] = ordered[y]
        for k, send in enumerate(sends, 1):
            send[...] = ordered[(y + k) % ny].astype(BF16)

    for_each(place[1], ny, hand_out)


def back_kernel(nz, ny, per_target, place, scale, w0, w1, w2, w3, *refs):
    gathered, (out, weights) = refs[:-2], refs[-2:]
    features, width = weights.shape
    own = features // (nz * ny)

    def arrange(here_y):
        for k, piece in enumerate((w0, w1, w2, w3)):
            y = (here_y - k) % ny
            for z in range(nz):
                at = (z * ny + y) * own
                weights[at : at + own, :] = piece[z].astype(F32)

    for_each(place[1], ny, arrange)
    slot_count = out.shape[0]
    step = 5 * BLOCK
    total = jnp.zeros((slot_count, width), F32)
    for rows in gathered:
        live = jnp.zeros((rows.shape[0], width), F32)
        for i in range(features // step):
            cut = slice(i * step, (i + 1) * step)
            scaled = (rows[:, cut].astype(F32) * scale[:, cut]).astype(BF16)
            live += jnp.dot(scaled, weights[cut, :].astype(BF16), preferred_element_type=F32)
        select = selection(rows[:, features:], per_target, slot_count)
        total += lax.dot_general(select, live.astype(BF16), ROWS_FIRST, preferred_element_type=F32)
    out[...] = total.astype(BF16)


def both_terms(value):
    high = value.astype(BF16).astype(F32)
    return jnp.concatenate([high, value - high], axis=0).astype(BF16)


def fold_y_kernel(nz, own, groups, place, kept, r1, r2, r3, by_z, near_kept, scale_kept, *rest):
    sends, (blocks, product, flat) = rest[:-3], rest[-3:]
    padded = product.shape[0] // nz
    width = product.shape[1]
    members = nz // groups
    total = kept[...]
    for part in (r1, r2, r3):
        total += part[...].astype(F32)
    product[...] = jnp.zeros_like(product)
    for z in range(nz):
        block = total[z * own : (z + 1) * own, :]
        blocks[z] = block
        weight = by_z[z].astype(F32)
        product[z * padded : z * padded + own, :] = block * weight
    rest = product[...]
    ones = jnp.ones((8, width), BF16)
    sums = jnp.zeros((8, nz * padded), F32)
    for _ in range(3):
        piece = rest.astype(BF16)
        rest = rest - piece.astype(F32)
        sums += lax.dot_general(ones, piece, LANES_LAST, preferred_element_type=F32)
    scale_kept[...] = jnp.zeros_like(scale_kept)
    for j in range(-(-nz * padded // width)):
        row = sums[0:1, j * width : (j + 1) * width]
        scale_kept[j : j + 1, : row.shape[1]] = row
    both = both_terms(scale_kept[...]).astype(F32)

    def hand_out(low):
        for h in range(groups):
            near_kept[h] = blocks[h * members + low]
        for k, send in enumerate(sends, 1):
            for h in range(groups):
                flat[h * own : (h + 1) * own, :] = blocks[h * members + (low + k) % members]
            flat[groups * own :, :] = both
            send[...] = flat[...].astype(BF16)

    for_each(lax.rem(place[0], members), members, hand_out)


def fold_low_kernel(near_kept, scale_kept, r1, r2, r3, out):
    groups, own, width = near_kept.shape
    lines = scale_kept.shape[0]
    parts = [part[...].astype(F32) for part in (r1, r2, r3)]
    scale = scale_kept[...]
    for part in parts:
        both = part[groups * own :]
        scale = scale + (both[:lines] + both[lines:])
    both = both_terms(scale).astype(F32)
    gap = jnp.zeros((out.shape[1] - own - 2 * lines, width), F32)
    for h in range(groups):
        total = near_kept[h]
        for part in parts:
            total += part[h * own : (h + 1) * own]
        out[h] = jnp.concatenate([total, gap, both], axis=0).astype(BF16)


def fold_high_kernel(factor, parts, gain, out, scale_out):
    total = parts[0].astype(F32)
    for h in range(1, parts.shape[0]):
        total += parts[h].astype(F32)
    own, lines = out.shape[0], scale_out.shape[1]
    out[...] = total[:own] * (gain[...] * factor)
    both = total[total.shape[0] - 2 * lines :]
    for k in range(scale_out.shape[0]):
        scale_out[k] = both[:lines] + both[lines:]


def spread_kernel(source, out):
    for k in range(out.shape[0]):
        out[k] = source[...]


def collect_kernel(place, *refs):
    parts, out = refs[:-1], refs[-1]
    count = len(parts)

    def place_all(here):
        for k, part in enumerate(parts):
            for z in range(out.shape[0]):
                out[z, (here - k) % count] = part[z]

    for_each(place[1], count, place_all)


def share_kernel(place, source, kept, *sends):
    count = source.shape[1]
    for k, out in enumerate((kept,) + sends):
        there = lax.rem(place[1] + k, count)
        for z in range(source.shape[0]):
            out[z] = source[z, there]


def unswap_kernel(owners, capacity, place, *refs):
    parts, (out, ordered) = refs[:-2], refs[-2:]
    ny, nz, width = len(parts), ordered.shape[0], ordered.shape[3]
    encoders = nz * ny
    for k, part in enumerate(parts):
        y = lax.rem(place[1] + ny - k, ny)
        for z in range(nz):
            ordered[z, y] = part[z]
    group = 8
    slab = group * capacity
    matrix = swap_matrix(group, owners, capacity, BF16)
    for g in range(encoders // group):
        picked = [ordered[(g * group + e) // ny, (g * group + e) % ny] for e in range(group)]
        moved = jnp.dot(matrix, jnp.concatenate(picked, axis=0), preferred_element_type=F32).astype(BF16)
        for l in range(owners):
            at = (l * encoders + g * group) * capacity
            out[at : at + slab, :] = moved[l * slab : (l + 1) * slab, :]


def shifted(value, axis, size, shift):
    return lax.ppermute(value, axis, [(i, (i + shift) % size) for i in range(size)])


def all_to_all(value, axes):
    return lax.all_to_all(value, axes, split_axis=0, concat_axis=0, tiled=True)


def on_device(grad_rows, row_target, stored_context, block_scale, w_out, layer_scale):
    nz, ny, nx, nc = (lax.axis_size(a) for a in (Z, "y", "x", "c"))
    encoders, owners = nz * ny, nx * nc
    source_rows, features = grad_rows.shape
    slot_count, width = stored_context.shape
    capacity = slot_count // (encoders * owners)
    own = features // encoders
    per_target = owners * capacity
    shape = jax.ShapeDtypeStruct
    owner = lax.axis_index(("x", "c")).reshape(1)
    place = jnp.stack([lax.axis_index(Z), lax.axis_index("y")])

    send = call(
        lambda *args: context_kernel(owners, encoders, capacity, *args),
        [shape((nz, per_target, width), BF16)] * ny, (place, stored_context, block_scale), flops=10**8, scalars=1,
        scratch=[pltpu.VMEM((ny, nz, per_target, width), BF16)],
    )
    weights = all_to_all(
        call(spread_kernel, shape((nz, own, width), BF16), (w_out.T,), flops=10**6), Z,
    )
    sent = [send[0]] + [shifted(part, "y", ny, k) for k, part in enumerate(send[1:], 1)]
    sent = call(
        collect_kernel, shape((nz, ny, per_target, width), BF16), (place, *sent), flops=10**8, scalars=1, after=(weights,),
    )
    slots = all_to_all(sent, Z).reshape(slot_count, width)

    wide = features + BLOCK
    mine = call(
        lambda *args: rows_kernel(capacity, *args),
        shape((source_rows, wide), BF16), (owner, grad_rows, row_target, row_target.reshape(1, source_rows)),
        flops=10**8, scalars=1, after=(send[0],),
    )
    near = call(
        stack_kernel, shape((nx * source_rows, wide), BF16), [mine] + [shifted(mine, "x", nx, k) for k in range(1, nx)],
        flops=10**8, after=(weights,),
    )
    rows = [near, shifted(near, "c", nc, 1)]
    pieces = [weights] + [shifted(weights, "y", ny, k) for k in range(1, ny)]

    share = nz * own
    kept, *sends = call(
        lambda *args: outer_kernel(nz, ny, per_target, *args),
        [shape((share, width), F32)] + [shape((share, width), BF16)] * (ny - 1),
        (place, slots, *rows), flops=10**9, scalars=1,
        scratch=[
            pltpu.VMEM((ny, share, width), F32),
        ],
    )
    parts = [shifted(send, "y", ny, k) for k, send in enumerate(sends, 1)]

    back = call(
        lambda *args: back_kernel(nz, ny, per_target, *args),
        shape((slot_count, width), BF16),
        (place, layer_scale.reshape(1, features), *pieces, *rows), flops=2 * 10**9, scalars=1, after=(kept,),
        scratch=[pltpu.VMEM((features, width), F32)],
    )
    returned = all_to_all(back.reshape(nz, ny, per_target, width), Z)
    sends = call(
        share_kernel, [shape((nz, per_target, width), BF16)] * ny, (place, returned), flops=10**8, scalars=1,
    )
    sends = [sends[0]] + [shifted(send, "y", ny, k) for k, send in enumerate(sends[1:], 1)]
    grad_context = call(
        lambda *args: unswap_kernel(owners, capacity, *args),
        shape((slot_count, width), BF16), (place, *sends), flops=10**8, scalars=1,
        scratch=[pltpu.VMEM((nz, ny, per_target, width), BF16)],
    )

    groups = lax.axis_size("h")
    members = nz // groups
    padded = -(-own // 8) * 8
    lines = -(-nz * padded // width)
    low, low_scale, *sends = call(
        lambda *args: fold_y_kernel(nz, own, groups, *args),
        [shape((groups, own, width), F32), shape((lines, width), F32)]
        + [shape((groups * own + 2 * lines, width), BF16)] * (members - 1),
        (place, kept, *parts, weights), flops=2 * 10**11, scalars=1,
        scratch=[
            pltpu.VMEM((nz, own, width), F32),
            pltpu.VMEM((nz * padded, width), F32),
            pltpu.VMEM((groups * own + 2 * lines, width), F32),
        ],
    )
    parts = [shifted(send, "l", members, k) for k, send in enumerate(sends, 1)]
    rows_sent = -(-(own + 2 * lines) // 16) * 16
    total = call(
        fold_low_kernel, shape((groups, rows_sent, width), BF16), (low, low_scale, *parts), flops=10**11, after=(returned,),
    )
    rescale = 1.0 / math.sqrt(source_rows * encoders * owners)
    at = lax.axis_index(Z + ("y",)) * own
    own_scale = lax.dynamic_slice(layer_scale, (at,), (own,))
    grad_weight, scale_part = call(
        lambda *args: fold_high_kernel(rescale, *args),
        [shape((own, width), F32), shape((ny * owners, lines, width), F32)],
        (all_to_all(total, "h"), own_scale.reshape(own, 1)), flops=10**8,
    )
    scale_part = all_to_all(scale_part, ("y", "x", "c")).reshape(ny, owners, lines * width)[:, :, : nz * padded]
    scale_part = jnp.sum(scale_part, axis=1).reshape(ny, nz, padded)[:, :, :own]
    grad_scale = scale_part.transpose(1, 0, 2).reshape(features) * rescale
    return (grad_context, grad_weight, grad_scale)


def solution(mesh):
    finer = Mesh(mesh.devices.reshape(4, 4, 4, 4, 2), Z + ("y", "x", "c"))
    edata, llm = Z + ("y",), ("x", "c")
    in_specs = (
        P(edata + llm, None),
        P(edata + llm, None),
        P(edata, llm),
        P(edata, llm),
        P(llm, edata),
        P(),
    )
    out_specs = (P(edata, llm), P(edata, llm), P())
    return jax.shard_map(
        on_device, mesh=finer, in_specs=in_specs, out_specs=out_specs, check_vma=False
    )
```

```python
import math

import jax
import jax.numpy as jnp
from jax import lax
from jax.experimental import pallas as pl
from jax.experimental.pallas import tpu as pltpu
from jax.sharding import Mesh
from jax.sharding import PartitionSpec as P

BLOCK = 128
F32 = jnp.float32
BF16 = jnp.bfloat16
I32 = jnp.int32
Z = ("h", "l")
ROWS_FIRST = (((0,), (0,)), ((), ()))
LANES_LAST = (((1,), (1,)), ((), ()))


def call(kernel, out_shape, args, flops, scalars=0, scratch=(), after=()):
    whole = pl.BlockSpec(memory_space=pltpu.VMEM)
    count, more = len(args), len(after)

    def body(*refs):
        kernel(*refs[:count], *refs[count + more :])

    specs = [pl.BlockSpec(memory_space=pltpu.SMEM)] * scalars + [whole] * (count - scalars)
    return pl.pallas_call(
        body,
        out_shape=out_shape,
        in_specs=specs + [pl.BlockSpec(memory_space=pl.ANY)] * more,
        out_specs=jax.tree.map(lambda _: whole, out_shape),
        scratch_shapes=list(scratch),
        compiler_params=pltpu.CompilerParams(vmem_limit_bytes=20 * 2**20),
        cost_estimate=pl.CostEstimate(flops=flops, bytes_accessed=4 * 2**20, transcendentals=0),
    )(*args, *after)


def for_each(index, count, body):
    for value in range(count):

        @pl.when(index == value)
        def _(value=value):
            body(value)


def swap_matrix(inner, outer, capacity, dtype):
    size = inner * outer * capacity
    row = lax.broadcasted_iota(I32, (size, size), 0)
    col = lax.broadcasted_iota(I32, (size, size), 1)
    o, i, a = row // (inner * capacity), (row // capacity) % inner, row % capacity
    return (col == (i * outer + o) * capacity + a).astype(dtype)


def context_kernel(owners, encoders, capacity, place, stored, scale, *refs):
    sends, send = refs[:-1], refs[-1]
    group = 8
    slab = group * capacity
    matrix = swap_matrix(owners, group, capacity, BF16)
    parts = []
    for b in range(scale.shape[1]):
        part = stored[:, b * BLOCK : (b + 1) * BLOCK].astype(F32) * scale[:, b : b + 1]
        parts.append(part.astype(BF16))
    context = jnp.concatenate(parts, axis=1)
    block = owners * capacity
    for g in range(encoders // group):
        picked = [context[(l * encoders + g * group) * capacity :][:slab] for l in range(owners)]
        moved = jnp.dot(matrix, jnp.concatenate(picked, axis=0), preferred_element_type=F32).astype(BF16)
        for e in range(group):
            z, y = divmod(g * group + e, send.shape[0])
            send[y, z] = moved[e * block : (e + 1) * block, :]
    for k, out in enumerate(sends):
        out[...] = send[lax.rem(place[1] + k, len(sends))]


def rows_kernel(capacity, own_owner, rows, target_col, target_row, mine):
    count, features = rows.shape
    earlier = lax.broadcasted_iota(I32, (count, count), 1) < lax.broadcasted_iota(I32, (count, count), 0)
    same = jnp.where((target_col[...] == target_row[...]) & earlier, 1.0, 0.0)
    arrival = jnp.sum(same, axis=1, keepdims=True)
    low = arrival + (own_owner[0] * capacity).astype(F32)
    lane = lax.broadcasted_iota(I32, (count, BLOCK), 1)
    tail = jnp.where(lane == 0, target_col[...].astype(F32), jnp.where(lane == 1, low, 0.0))
    mine[:, :features] = rows[...]
    mine[:, features:] = tail.astype(BF16)


def stack_kernel(*refs):
    out, count = refs[-1], refs[0].shape[0]
    for k, ref in enumerate(refs[:-1]):
        out[k * count : (k + 1) * count, :] = ref[...]


def selection(tail, per_target, slot_count):
    tail = tail.astype(F32)
    slot = (tail[:, 0:1] * per_target + tail[:, 1:2]).astype(I32)
    lanes = lax.broadcasted_iota(I32, (tail.shape[0], slot_count), 1)
    return (lanes == slot).astype(BF16)


def outer_kernel(nz, ny, per_target, place, slots, *refs):
    gathered, (kept, *sends), ordered = refs[: -ny - 1], refs[-ny - 1 : -1], refs[-1]
    share, width = kept.shape
    features, own = share * ny, share // nz
    selects = [selection(rows[:, features:], per_target, slots.shape[0]) for rows in gathered]
    contexts = [jnp.dot(select, slots[...], preferred_element_type=F32).astype(BF16) for select in selects]
    step = 5 * BLOCK
    for at in range(0, features, step):
        part = 0.0
        for rows, context in zip(gathered, contexts):
            part += lax.dot_general(rows[:, at : at + step], context, ROWS_FIRST, preferred_element_type=F32)
        first = at
        while first < at + step:
            block, row = divmod(first, own)
            count = min(own - row, at + step - first)
            z, y = divmod(block, ny)
            ordered[y, z * own + row : z * own + row + count, :] = part[first - at : first - at + count, :]
            first += count

    def hand_out(y):
        kept[...] = ordered[y]
        for k, send in enumerate(sends, 1):
            send[...] = ordered[(y + k) % ny].astype(BF16)

    for_each(place[1], ny, hand_out)


def back_kernel(nz, ny, per_target, place, scale, w0, w1, w2, w3, *refs):
    gathered, (out, weights) = refs[:-2], refs[-2:]
    features, width = weights.shape
    own = features // (nz * ny)

    def arrange(here_y):
        for k, piece in enumerate((w0, w1, w2, w3)):
            y = (here_y - k) % ny
            for z in range(nz):
                at = (z * ny + y) * own
                weights[at : at + own, :] = piece[z].astype(F32)

    for_each(place[1], ny, arrange)
    slot_count = out.shape[0]
    step = 5 * BLOCK
    total = jnp.zeros((slot_count, width), F32)
    for rows in gathered:
        live = jnp.zeros((rows.shape[0], width), F32)
        for i in range(features // step):
            cut = slice(i * step, (i + 1) * step)
            scaled = (rows[:, cut].astype(F32) * scale[:, cut]).astype(BF16)
            live += jnp.dot(scaled, weights[cut, :].astype(BF16), preferred_element_type=F32)
        select = selection(rows[:, features:], per_target, slot_count)
        total += lax.dot_general(select, live.astype(BF16), ROWS_FIRST, preferred_element_type=F32)
    out[...] = total.astype(BF16)


def both_terms(value):
    high = value.astype(BF16).astype(F32)
    return jnp.concatenate([high, value - high], axis=0).astype(BF16)


def fold_y_kernel(nz, own, groups, place, kept, r1, r2, r3, by_z, near_kept, scale_kept, *rest):
    sends, (blocks, product, flat) = rest[:-3], rest[-3:]
    padded = product.shape[0] // nz
    width = product.shape[1]
    members = nz // groups
    total = kept[...]
    for part in (r1, r2, r3):
        total += part[...].astype(F32)
    product[...] = jnp.zeros_like(product)
    for z in range(nz):
        block = total[z * own : (z + 1) * own, :]
        blocks[z] = block
        weight = by_z[z].astype(F32)
        product[z * padded : z * padded + own, :] = block * weight
    rest = product[...]
    ones = jnp.ones((8, width), BF16)
    sums = jnp.zeros((8, nz * padded), F32)
    for _ in range(3):
        piece = rest.astype(BF16)
        rest = rest - piece.astype(F32)
        sums += lax.dot_general(ones, piece, LANES_LAST, preferred_element_type=F32)
    scale_kept[...] = jnp.zeros_like(scale_kept)
    for j in range(-(-nz * padded // width)):
        row = sums[0:1, j * width : (j + 1) * width]
        scale_kept[j : j + 1, : row.shape[1]] = row
    both = both_terms(scale_kept[...]).astype(F32)

    def hand_out(low):
        for h in range(groups):
            near_kept[h] = blocks[h * members + low]
        for k, send in enumerate(sends, 1):
            for h in range(groups):
                flat[h * own : (h + 1) * own, :] = blocks[h * members + (low + k) % members]
            flat[groups * own :, :] = both
            send[...] = flat[...].astype(BF16)

    for_each(lax.rem(place[0], members), members, hand_out)


def fold_low_kernel(near_kept, scale_kept, r1, r2, r3, out):
    groups, own, width = near_kept.shape
    lines = scale_kept.shape[0]
    parts = [part[...].astype(F32) for part in (r1, r2, r3)]
    scale = scale_kept[...]
    for part in parts:
        both = part[groups * own :]
        scale = scale + (both[:lines] + both[lines:])
    both = both_terms(scale).astype(F32)
    gap = jnp.zeros((out.shape[1] - own - 2 * lines, width), F32)
    for h in range(groups):
        total = near_kept[h]
        for part in parts:
            total += part[h * own : (h + 1) * own]
        out[h] = jnp.concatenate([total, gap, both], axis=0).astype(BF16)


def fold_high_kernel(factor, parts, gain, out, scale_out):
    total = parts[0].astype(F32)
    for h in range(1, parts.shape[0]):
        total += parts[h].astype(F32)
    own, lines = out.shape[0], scale_out.shape[1]
    out[...] = total[:own] * (gain[...] * factor)
    both = total[total.shape[0] - 2 * lines :]
    for k in range(scale_out.shape[0]):
        scale_out[k] = both[:lines] + both[lines:]


def spread_kernel(source, out):
    for k in range(out.shape[0]):
        out[k] = source[...]


def collect_kernel(place, *refs):
    parts, out = refs[:-1], refs[-1]
    count = len(parts)

    def place_all(here):
        for k, part in enumerate(parts):
            for z in range(out.shape[0]):
                out[z, (here - k) % count] = part[z]

    for_each(place[1], count, place_all)


def share_kernel(place, source, kept, *sends):
    count = source.shape[1]
    for k, out in enumerate((kept,) + sends):
        there = lax.rem(place[1] + k, count)
        for z in range(source.shape[0]):
            out[z] = source[z, there]


def unswap_kernel(owners, capacity, place, *refs):
    parts, (out, ordered) = refs[:-2], refs[-2:]
    ny, nz, width = len(parts), ordered.shape[0], ordered.shape[3]
    encoders = nz * ny
    for k, part in enumerate(parts):
        y = lax.rem(place[1] + ny - k, ny)
        for z in range(nz):
            ordered[z, y] = part[z]
    group = 8
    slab = group * capacity
    matrix = swap_matrix(group, owners, capacity, BF16)
    for g in range(encoders // group):
        picked = [ordered[(g * group + e) // ny, (g * group + e) % ny] for e in range(group)]
        moved = jnp.dot(matrix, jnp.concatenate(picked, axis=0), preferred_element_type=F32).astype(BF16)
        for l in range(owners):
            at = (l * encoders + g * group) * capacity
            out[at : at + slab, :] = moved[l * slab : (l + 1) * slab, :]


def shifted(value, axis, size, shift):
    return lax.ppermute(value, axis, [(i, (i + shift) % size) for i in range(size)])


def all_to_all(value, axes):
    return lax.all_to_all(value, axes, split_axis=0, concat_axis=0, tiled=True)


def on_device(grad_rows, row_target, stored_context, block_scale, w_out, layer_scale):
    nz, ny, nx, nc = (lax.axis_size(a) for a in (Z, "y", "x", "c"))
    encoders, owners = nz * ny, nx * nc
    source_rows, features = grad_rows.shape
    slot_count, width = stored_context.shape
    capacity = slot_count // (encoders * owners)
    own = features // encoders
    per_target = owners * capacity
    shape = jax.ShapeDtypeStruct
    owner = lax.axis_index(("x", "c")).reshape(1)
    place = jnp.stack([lax.axis_index(Z), lax.axis_index("y")])

    send = call(
        lambda *args: context_kernel(owners, encoders, capacity, *args),
        [shape((nz, per_target, width), BF16)] * ny, (place, stored_context, block_scale), flops=10**8, scalars=1,
        scratch=[pltpu.VMEM((ny, nz, per_target, width), BF16)],
    )
    weights = all_to_all(
        call(spread_kernel, shape((nz, own, width), BF16), (w_out.T,), flops=10**6), Z,
    )
    sent = [send[0]] + [shifted(part, "y", ny, k) for k, part in enumerate(send[1:], 1)]
    received = sent[1:]
    sent = call(
        collect_kernel, shape((nz, ny, per_target, width), BF16), (place, *sent), flops=10**8, scalars=1, after=(weights,),
    )
    slots = all_to_all(sent, Z).reshape(slot_count, width)

    wide = features + BLOCK
    mine = call(
        lambda *args: rows_kernel(capacity, *args),
        shape((source_rows, wide), BF16), (owner, grad_rows, row_target, row_target.reshape(1, source_rows)),
        flops=10**8, scalars=1, after=(send[0],),
    )
    late = call(stack_kernel, shape((source_rows, wide), BF16), [mine], flops=10**6, after=received)
    near = call(
        stack_kernel, shape((nx * source_rows, wide), BF16), [mine] + [shifted(mine if k < nx - 1 else late, "x", nx, k) for k in range(1, nx)],
        flops=10**8, after=(weights,),
    )
    rows = [near, shifted(near, "c", nc, 1)]
    pieces = [weights] + [shifted(weights, "y", ny, k) for k in range(1, ny)]

    share = nz * own
    kept, *sends = call(
        lambda *args: outer_kernel(nz, ny, per_target, *args),
        [shape((share, width), F32)] + [shape((share, width), BF16)] * (ny - 1),
        (place, slots, *rows), flops=10**9, scalars=1,
        scratch=[
            pltpu.VMEM((ny, share, width), F32),
        ],
    )
    parts = [shifted(send, "y", ny, k) for k, send in enumerate(sends, 1)]

    back = call(
        lambda *args: back_kernel(nz, ny, per_target, *args),
        shape((slot_count, width), BF16),
        (place, layer_scale.reshape(1, features), *pieces, *rows), flops=2 * 10**9, scalars=1, after=(kept,),
        scratch=[pltpu.VMEM((features, width), F32)],
    )
    returned = all_to_all(back.reshape(nz, ny, per_target, width), Z)
    sends = call(
        share_kernel, [shape((nz, per_target, width), BF16)] * ny, (place, returned), flops=10**8, scalars=1,
    )
    sends = [sends[0]] + [shifted(send, "y", ny, k) for k, send in enumerate(sends[1:], 1)]
    grad_context = call(
        lambda *args: unswap_kernel(owners, capacity, *args),
        shape((slot_count, width), BF16), (place, *sends), flops=10**8, scalars=1,
        scratch=[pltpu.VMEM((nz, ny, per_target, width), BF16)],
    )

    groups = lax.axis_size("h")
    members = nz // groups
    padded = -(-own // 8) * 8
    lines = -(-nz * padded // width)
    low, low_scale, *sends = call(
        lambda *args: fold_y_kernel(nz, own, groups, *args),
        [shape((groups, own, width), F32), shape((lines, width), F32)]
        + [shape((groups * own + 2 * lines, width), BF16)] * (members - 1),
        (place, kept, *parts, weights), flops=2 * 10**11, scalars=1,
        scratch=[
            pltpu.VMEM((nz, own, width), F32),
            pltpu.VMEM((nz * padded, width), F32),
            pltpu.VMEM((groups * own + 2 * lines, width), F32),
        ],
    )
    parts = [shifted(send, "l", members, k) for k, send in enumerate(sends, 1)]
    rows_sent = -(-(own + 2 * lines) // 16) * 16
    total = call(
        fold_low_kernel, shape((groups, rows_sent, width), BF16), (low, low_scale, *parts), flops=10**11, after=(returned,),
    )
    rescale = 1.0 / math.sqrt(source_rows * encoders * owners)
    at = lax.axis_index(Z + ("y",)) * own
    own_scale = lax.dynamic_slice(layer_scale, (at,), (own,))
    grad_weight, scale_part = call(
        lambda *args: fold_high_kernel(rescale, *args),
        [shape((own, width), F32), shape((ny * owners, lines, width), F32)],
        (all_to_all(total, "h"), own_scale.reshape(own, 1)), flops=10**8,
    )
    scale_part = all_to_all(scale_part, ("y", "x", "c")).reshape(ny, owners, lines * width)[:, :, : nz * padded]
    scale_part = jnp.sum(scale_part, axis=1).reshape(ny, nz, padded)[:, :, :own]
    grad_scale = scale_part.transpose(1, 0, 2).reshape(features) * rescale
    return (grad_context, grad_weight, grad_scale)


def solution(mesh):
    finer = Mesh(mesh.devices.reshape(4, 4, 4, 4, 2), Z + ("y", "x", "c"))
    edata, llm = Z + ("y",), ("x", "c")
    in_specs = (
        P(edata + llm, None),
        P(edata + llm, None),
        P(edata, llm),
        P(edata, llm),
        P(llm, edata),
        P(),
    )
    out_specs = (P(edata, llm), P(edata, llm), P())
    return jax.shard_map(
        on_device, mesh=finer, in_specs=in_specs, out_specs=out_specs, check_vma=False
    )
```

```python
import math

import jax
import jax.numpy as jnp
from jax import lax
from jax.experimental import pallas as pl
from jax.experimental.pallas import tpu as pltpu
from jax.sharding import Mesh
from jax.sharding import PartitionSpec as P

BLOCK = 128
F32 = jnp.float32
BF16 = jnp.bfloat16
I32 = jnp.int32
Z = ("h", "l")
ROWS_FIRST = (((0,), (0,)), ((), ()))
LANES_LAST = (((1,), (1,)), ((), ()))


def call(kernel, out_shape, args, flops, scalars=0, scratch=(), after=()):
    whole = pl.BlockSpec(memory_space=pltpu.VMEM)
    count, more = len(args), len(after)

    def body(*refs):
        kernel(*refs[:count], *refs[count + more :])

    specs = [pl.BlockSpec(memory_space=pltpu.SMEM)] * scalars + [whole] * (count - scalars)
    return pl.pallas_call(
        body,
        out_shape=out_shape,
        in_specs=specs + [pl.BlockSpec(memory_space=pl.ANY)] * more,
        out_specs=jax.tree.map(lambda _: whole, out_shape),
        scratch_shapes=list(scratch),
        compiler_params=pltpu.CompilerParams(vmem_limit_bytes=16 * 2**20),
        cost_estimate=pl.CostEstimate(flops=flops, bytes_accessed=4 * 2**20, transcendentals=0),
    )(*args, *after)


def for_each(index, count, body):
    for value in range(count):

        @pl.when(index == value)
        def _(value=value):
            body(value)


def swap_matrix(inner, outer, capacity, dtype):
    size = inner * outer * capacity
    row = lax.broadcasted_iota(I32, (size, size), 0)
    col = lax.broadcasted_iota(I32, (size, size), 1)
    o, i, a = row // (inner * capacity), (row // capacity) % inner, row % capacity
    return (col == (i * outer + o) * capacity + a).astype(dtype)


def context_kernel(owners, encoders, capacity, place, stored, scale, *refs):
    sends, send = refs[:-1], refs[-1]
    group = 8
    slab = group * capacity
    matrix = swap_matrix(owners, group, capacity, BF16)
    parts = []
    for b in range(scale.shape[1]):
        part = stored[:, b * BLOCK : (b + 1) * BLOCK].astype(F32) * scale[:, b : b + 1]
        parts.append(part.astype(BF16))
    context = jnp.concatenate(parts, axis=1)
    block = owners * capacity
    for g in range(encoders // group):
        picked = [context[(l * encoders + g * group) * capacity :][:slab] for l in range(owners)]
        moved = jnp.dot(matrix, jnp.concatenate(picked, axis=0), preferred_element_type=F32).astype(BF16)
        for e in range(group):
            z, y = divmod(g * group + e, send.shape[0])
            send[y, z] = moved[e * block : (e + 1) * block, :]
    for k, out in enumerate(sends):
        out[...] = send[lax.rem(place[1] + k, len(sends))]


def rows_kernel(capacity, own_owner, rows, target_col, target_row, mine):
    count, features = rows.shape
    earlier = lax.broadcasted_iota(I32, (count, count), 1) < lax.broadcasted_iota(I32, (count, count), 0)
    same = jnp.where((target_col[...] == target_row[...]) & earlier, 1.0, 0.0)
    arrival = jnp.sum(same, axis=1, keepdims=True)
    low = arrival + (own_owner[0] * capacity).astype(F32)
    lane = lax.broadcasted_iota(I32, (count, BLOCK), 1)
    tail = jnp.where(lane == 0, target_col[...].astype(F32), jnp.where(lane == 1, low, 0.0))
    mine[:, :features] = rows[...]
    mine[:, features:] = tail.astype(BF16)


def stack_kernel(*refs):
    out, count = refs[-1], refs[0].shape[0]
    for k, ref in enumerate(refs[:-1]):
        out[k * count : (k + 1) * count, :] = ref[...]


def selection(tail, per_target, slot_count):
    tail = tail.astype(F32)
    slot = (tail[:, 0:1] * per_target + tail[:, 1:2]).astype(I32)
    lanes = lax.broadcasted_iota(I32, (tail.shape[0], slot_count), 1)
    return (lanes == slot).astype(BF16)


def outer_kernel(nz, ny, per_target, place, slots, *refs):
    gathered, (kept, *sends), ordered = refs[: -ny - 1], refs[-ny - 1 : -1], refs[-1]
    share, width = kept.shape
    features, own = share * ny, share // nz
    selects = [selection(rows[:, features:], per_target, slots.shape[0]) for rows in gathered]
    contexts = [jnp.dot(select, slots[...], preferred_element_type=F32).astype(BF16) for select in selects]
    step = 5 * BLOCK
    for at in range(0, features, step):
        part = 0.0
        for rows, context in zip(gathered, contexts):
            part += lax.dot_general(rows[:, at : at + step], context, ROWS_FIRST, preferred_element_type=F32)
        first = at
        while first < at + step:
            block, row = divmod(first, own)
            count = min(own - row, at + step - first)
            z, y = divmod(block, ny)
            ordered[y, z * own + row : z * own + row + count, :] = part[first - at : first - at + count, :]
            first += count

    def hand_out(y):
        kept[...] = ordered[y]
        for k, send in enumerate(sends, 1):
            send[...] = ordered[(y + k) % ny].astype(BF16)

    for_each(place[1], ny, hand_out)


def back_kernel(nz, ny, per_target, place, scale, w0, w1, w2, w3, *refs):
    gathered, (out, weights) = refs[:-2], refs[-2:]
    features, width = weights.shape
    own = features // (nz * ny)

    def arrange(here_y):
        for k, piece in enumerate((w0, w1, w2, w3)):
            y = (here_y - k) % ny
            for z in range(nz):
                at = (z * ny + y) * own
                weights[at : at + own, :] = piece[z].astype(F32)

    for_each(place[1], ny, arrange)
    slot_count = out.shape[0]
    step = 5 * BLOCK
    total = jnp.zeros((slot_count, width), F32)
    for rows in gathered:
        live = jnp.zeros((rows.shape[0], width), F32)
        for i in range(features // step):
            cut = slice(i * step, (i + 1) * step)
            scaled = (rows[:, cut].astype(F32) * scale[:, cut]).astype(BF16)
            live += jnp.dot(scaled, weights[cut, :].astype(BF16), preferred_element_type=F32)
        select = selection(rows[:, features:], per_target, slot_count)
        total += lax.dot_general(select, live.astype(BF16), ROWS_FIRST, preferred_element_type=F32)
    out[...] = total.astype(BF16)


def both_terms(value):
    high = value.astype(BF16).astype(F32)
    return jnp.concatenate([high, value - high], axis=0).astype(BF16)


def fold_y_kernel(nz, own, groups, place, kept, r1, r2, r3, by_z, near_kept, scale_kept, *rest):
    sends, (blocks, product, flat) = rest[:-3], rest[-3:]
    padded = product.shape[0] // nz
    width = product.shape[1]
    members = nz // groups
    total = kept[...]
    for part in (r1, r2, r3):
        total += part[...].astype(F32)
    product[...] = jnp.zeros_like(product)
    for z in range(nz):
        block = total[z * own : (z + 1) * own, :]
        blocks[z] = block
        weight = by_z[z].astype(F32)
        product[z * padded : z * padded + own, :] = block * weight
    rest = product[...]
    ones = jnp.ones((8, width), BF16)
    sums = jnp.zeros((8, nz * padded), F32)
    for _ in range(3):
        piece = rest.astype(BF16)
        rest = rest - piece.astype(F32)
        sums += lax.dot_general(ones, piece, LANES_LAST, preferred_element_type=F32)
    scale_kept[...] = jnp.zeros_like(scale_kept)
    for j in range(-(-nz * padded // width)):
        row = sums[0:1, j * width : (j + 1) * width]
        scale_kept[j : j + 1, : row.shape[1]] = row
    both = both_terms(scale_kept[...]).astype(F32)

    def hand_out(low):
        for h in range(groups):
            near_kept[h] = blocks[h * members + low]
        for k, send in enumerate(sends, 1):
            for h in range(groups):
                flat[h * own : (h + 1) * own, :] = blocks[h * members + (low + k) % members]
            flat[groups * own :, :] = both
            send[...] = flat[...].astype(BF16)

    for_each(lax.rem(place[0], members), members, hand_out)


def fold_low_kernel(near_kept, scale_kept, r1, r2, r3, out):
    groups, own, width = near_kept.shape
    lines = scale_kept.shape[0]
    parts = [part[...].astype(F32) for part in (r1, r2, r3)]
    scale = scale_kept[...]
    for part in parts:
        both = part[groups * own :]
        scale = scale + (both[:lines] + both[lines:])
    both = both_terms(scale).astype(F32)
    gap = jnp.zeros((out.shape[1] - own - 2 * lines, width), F32)
    for h in range(groups):
        total = near_kept[h]
        for part in parts:
            total += part[h * own : (h + 1) * own]
        out[h] = jnp.concatenate([total, gap, both], axis=0).astype(BF16)


def fold_high_kernel(factor, parts, gain, out, scale_out):
    total = parts[0].astype(F32)
    for h in range(1, parts.shape[0]):
        total += parts[h].astype(F32)
    own, lines = out.shape[0], scale_out.shape[1]
    out[...] = total[:own] * (gain[...] * factor)
    both = total[total.shape[0] - 2 * lines :]
    for k in range(scale_out.shape[0]):
        scale_out[k] = both[:lines] + both[lines:]


def spread_kernel(source, out):
    for k in range(out.shape[0]):
        out[k] = source[...]


def collect_kernel(place, *refs):
    parts, out = refs[:-1], refs[-1]
    count = len(parts)

    def place_all(here):
        for k, part in enumerate(parts):
            for z in range(out.shape[0]):
                out[z, (here - k) % count] = part[z]

    for_each(place[1], count, place_all)


def share_kernel(place, source, kept, *sends):
    count = source.shape[1]
    for k, out in enumerate((kept,) + sends):
        there = lax.rem(place[1] + k, count)
        for z in range(source.shape[0]):
            out[z] = source[z, there]


def unswap_kernel(owners, capacity, place, *refs):
    parts, (out, ordered) = refs[:-2], refs[-2:]
    ny, nz, width = len(parts), ordered.shape[0], ordered.shape[3]
    encoders = nz * ny
    for k, part in enumerate(parts):
        y = lax.rem(place[1] + ny - k, ny)
        for z in range(nz):
            ordered[z, y] = part[z]
    group = 8
    slab = group * capacity
    matrix = swap_matrix(group, owners, capacity, BF16)
    for g in range(encoders // group):
        picked = [ordered[(g * group + e) // ny, (g * group + e) % ny] for e in range(group)]
        moved = jnp.dot(matrix, jnp.concatenate(picked, axis=0), preferred_element_type=F32).astype(BF16)
        for l in range(owners):
            at = (l * encoders + g * group) * capacity
            out[at : at + slab, :] = moved[l * slab : (l + 1) * slab, :]


def shifted(value, axis, size, shift):
    return lax.ppermute(value, axis, [(i, (i + shift) % size) for i in range(size)])


def all_to_all(value, axes):
    return lax.all_to_all(value, axes, split_axis=0, concat_axis=0, tiled=True)


def on_device(grad_rows, row_target, stored_context, block_scale, w_out, layer_scale):
    nz, ny, nx, nc = (lax.axis_size(a) for a in (Z, "y", "x", "c"))
    encoders, owners = nz * ny, nx * nc
    source_rows, features = grad_rows.shape
    slot_count, width = stored_context.shape
    capacity = slot_count // (encoders * owners)
    own = features // encoders
    per_target = owners * capacity
    shape = jax.ShapeDtypeStruct
    owner = lax.axis_index(("x", "c")).reshape(1)
    place = jnp.stack([lax.axis_index(Z), lax.axis_index("y")])

    send = call(
        lambda *args: context_kernel(owners, encoders, capacity, *args),
        [shape((nz, per_target, width), BF16)] * ny, (place, stored_context, block_scale), flops=10**8, scalars=1,
        scratch=[pltpu.VMEM((ny, nz, per_target, width), BF16)],
    )
    weights = all_to_all(
        call(spread_kernel, shape((nz, own, width), BF16), (w_out.T,), flops=10**6), Z,
    )
    sent = [send[0]] + [shifted(part, "y", ny, k) for k, part in enumerate(send[1:], 1)]
    received = sent[1:]
    sent = call(
        collect_kernel, shape((nz, ny, per_target, width), BF16), (place, *sent), flops=10**8, scalars=1, after=(weights,),
    )
    slots = all_to_all(sent, Z).reshape(slot_count, width)

    wide = features + BLOCK
    mine = call(
        lambda *args: rows_kernel(capacity, *args),
        shape((source_rows, wide), BF16), (owner, grad_rows, row_target, row_target.reshape(1, source_rows)),
        flops=10**8, scalars=1, after=(send[0],),
    )
    late = call(stack_kernel, shape((source_rows, wide), BF16), [mine], flops=10**6, after=received)
    near = call(
        stack_kernel, shape((nx * source_rows, wide), BF16), [mine] + [shifted(mine if k < nx - 1 else late, "x", nx, k) for k in range(1, nx)],
        flops=10**8, after=(weights,),
    )
    rows = [near, shifted(near, "c", nc, 1)]
    pieces = [weights] + [shifted(weights, "y", ny, k) for k in range(1, ny)]

    share = nz * own
    kept, *sends = call(
        lambda *args: outer_kernel(nz, ny, per_target, *args),
        [shape((share, width), F32)] + [shape((share, width), BF16)] * (ny - 1),
        (place, slots, *rows), flops=10**9, scalars=1,
        scratch=[
            pltpu.VMEM((ny, share, width), F32),
        ],
    )
    parts = [shifted(send, "y", ny, k) for k, send in enumerate(sends, 1)]

    back = call(
        lambda *args: back_kernel(nz, ny, per_target, *args),
        shape((slot_count, width), BF16),
        (place, layer_scale.reshape(1, features), *pieces, *rows), flops=2 * 10**9, scalars=1, after=(kept,),
        scratch=[pltpu.VMEM((features, width), F32)],
    )
    returned = all_to_all(back.reshape(nz, ny, per_target, width), Z)
    sends = call(
        share_kernel, [shape((nz, per_target, width), BF16)] * ny, (place, returned), flops=10**8, scalars=1,
    )
    sends = [sends[0]] + [shifted(send, "y", ny, k) for k, send in enumerate(sends[1:], 1)]
    grad_context = call(
        lambda *args: unswap_kernel(owners, capacity, *args),
        shape((slot_count, width), BF16), (place, *sends), flops=10**8, scalars=1,
        scratch=[pltpu.VMEM((nz, ny, per_target, width), BF16)],
    )

    groups = lax.axis_size("h")
    members = nz // groups
    padded = -(-own // 8) * 8
    lines = -(-nz * padded // width)
    low, low_scale, *sends = call(
        lambda *args: fold_y_kernel(nz, own, groups, *args),
        [shape((groups, own, width), F32), shape((lines, width), F32)]
        + [shape((groups * own + 2 * lines, width), BF16)] * (members - 1),
        (place, kept, *parts, weights), flops=2 * 10**11, scalars=1,
        scratch=[
            pltpu.VMEM((nz, own, width), F32),
            pltpu.VMEM((nz * padded, width), F32),
            pltpu.VMEM((groups * own + 2 * lines, width), F32),
        ],
    )
    parts = [shifted(send, "l", members, k) for k, send in enumerate(sends, 1)]
    rows_sent = -(-(own + 2 * lines) // 16) * 16
    total = call(
        fold_low_kernel, shape((groups, rows_sent, width), BF16), (low, low_scale, *parts), flops=10**11, after=(returned,),
    )
    rescale = 1.0 / math.sqrt(source_rows * encoders * owners)
    at = lax.axis_index(Z + ("y",)) * own
    own_scale = lax.dynamic_slice(layer_scale, (at,), (own,))
    grad_weight, scale_part = call(
        lambda *args: fold_high_kernel(rescale, *args),
        [shape((own, width), F32), shape((ny * owners, lines, width), F32)],
        (all_to_all(total, "h"), own_scale.reshape(own, 1)), flops=10**8,
    )
    scale_part = all_to_all(scale_part, ("y", "x", "c")).reshape(ny, owners, lines * width)[:, :, : nz * padded]
    scale_part = jnp.sum(scale_part, axis=1).reshape(ny, nz, padded)[:, :, :own]
    grad_scale = scale_part.transpose(1, 0, 2).reshape(features) * rescale
    return (grad_context, grad_weight, grad_scale)


def solution(mesh):
    finer = Mesh(mesh.devices.reshape(4, 4, 4, 4, 2), Z + ("y", "x", "c"))
    edata, llm = Z + ("y",), ("x", "c")
    in_specs = (
        P(edata + llm, None),
        P(edata + llm, None),
        P(edata, llm),
        P(edata, llm),
        P(llm, edata),
        P(),
    )
    out_specs = (P(edata, llm), P(edata, llm), P())
    return jax.shard_map(
        on_device, mesh=finer, in_specs=in_specs, out_specs=out_specs, check_vma=False
    )
```
